256 devices in a mesh: ab: 4 (over y), cd: 64 (over x, z, core).
Axes of the slice: x: 4, y: 4, z: 8, core: 2. Of those that a mesh axis runs over, the one named last changes fastest.
Arguments:
- ladder_ints: bfloat16 [8, 12288, 12288], P(None, 'cd', 'ab'), may hold values from -0.15625 to 0.15625
- amplitudes: bfloat16 [2048, 12288], P('ab', 'cd'), may hold values from -6 to 6
- group_sizes: int32 [8], replicated, may hold values from 1 to 768, 2048 in all
- occ_energy: float32 [2048], replicated, may hold values from -2.5 to -0.5
- vir_energy: float32 [8, 12288], replicated, may hold values from 0.5 to 6
Outputs:
- increment: bfloat16 [2048, 12288], P(None, ('ab', 'cd'))
The draws below stay inside these ranges and needn't reach their ends.
Inputs may be any that keep to these rules, and one draw needn't show every extreme that they name: Group g holds the group_sizes[g] consecutive rows after those of groups 0 to g - 1; the sizes sum to 2048 and the largest is exactly 768.
All inputs are finite; a program needn't handle non-finite values.
Results may differ from the reference program's by a relative error of at most 0.0011.
Values may be sent and summed in bfloat16 or wider, within the bound.
No kernel may reach another device: no remote copies, remote signals or barrier semaphores. Data moves between devices by JAX's collectives and lax.ppermute only.
A program may use at most 192 MiB of HBM per device.

```python
import math
import jax
import jax.numpy as jnp
import numpy as np
from jax import lax

NIRREP = 8
NB = 12288
IJ = 2048
BLOCK = 128
MOST = 768


def spiked(array, stream_key, source, target, shards_of, factor):
    def block_of(axis_at):
        return (jnp.arange(array.shape[axis_at]) // (array.shape[axis_at] // shards_of)).reshape((-1,) + (1,) * (array.ndim - 1 - axis_at))

    near = jax.random.permutation(stream_key, shards_of)[block_of(target)]
    far = (block_of(target) + shards_of // 2) % shards_of
    return jnp.where((block_of(source) == near) | (block_of(source) == far), factor * array, array)


def levels(key, shape, cuts, smallest, largest):
    loudness, own = 1.0, jax.random.fold_in(key, 6)
    for dim, parts in cuts:
        draws = jnp.exp(jax.random.uniform(jax.random.fold_in(own, dim), (parts,), jnp.float32, smallest / len(cuts), largest / len(cuts)))
        loudness = loudness * jnp.repeat(draws, shape[dim] // parts).reshape([-1 if axis == dim else 1 for axis in range(len(shape))])
    return loudness


def split_up(number_of, total, most, skew):
    portions = [(1 << 20) // math.isqrt(rank ** skew) + 1 for rank in range(2, number_of + 1)]
    spare, given = total - most - (number_of - 1), [1] * (number_of - 1)
    while spare > 0:
        free = [i for i in range(number_of - 1) if given[i] < most]
        whole, remaining = sum([portions[i] for i in free]), spare
        for i in free:
            addition = min(most - given[i], max(1, remaining * portions[i] // whole), spare)
            given[i] = given[i] + addition
            spare = spare - addition
    return np.array([most] + given)


def ragged(own_key, number_of, total, most, skew):
    if number_of == 2:
        one = jax.random.randint(own_key, (), max(1, total - most), min(most, total - 1) + 1)
        return jnp.stack([one, total - one])
    lengths = jnp.asarray(split_up(number_of, total, most, skew), jnp.int32)
    pairs = (number_of - 1) // 2
    donor, receiver = lengths[1:1 + 2 * pairs:2], lengths[2:2 + 2 * pairs:2]
    margin = jnp.minimum(donor - 1, most - receiver)
    moved = jax.random.randint(jax.random.fold_in(own_key, 1), (pairs,), 0, 1 << 20) % (margin + 1)
    lengths = lengths.at[1:1 + 2 * pairs:2].set(donor - moved).at[2:2 + 2 * pairs:2].set(receiver + moved)
    return lengths[jax.random.permutation(jax.random.fold_in(own_key, 2), number_of)]


def gaussian(stream_key, extent, spread, most, cuts=(), held_as=jnp.bfloat16):
    values = jax.random.normal(stream_key, extent, jnp.float32) * spread
    if len(cuts) > 0:
        values = levels(stream_key, extent, cuts, -0.22, 0.18) * values
    return jnp.clip(values, min=-most, max=most).astype(held_as)


def bell_draw_with(stream_key, dims, spread, reach, cuts, heavy, kind=jnp.bfloat16):
    result = spread * jax.random.normal(stream_key, dims, jnp.float32)
    if cuts:
        result = result * levels(stream_key, dims, cuts, -0.22, 0.18)
    return jnp.clip(spiked(result, jax.random.fold_in(stream_key, 3), *heavy), -reach, reach).astype(kind)


def setup_inputs(seed: int = 0) -> dict:
    key_list = jax.random.split(jax.random.key(seed), 6)
    return {
        "ladder_ints": bell_draw_with(key_list[0], (NIRREP, NB, NB), NB ** -0.5, 0.15625, ((1, 64), (2, 4)), (1, 2, 64, 4.0)),
        "amplitudes": gaussian(key_list[1], (IJ, NB), 1.0, 6.0, ((0, 4), (1, 64))),
        "group_sizes": ragged(key_list[2], NIRREP, IJ, MOST, 1).astype(jnp.int32),
        "occ_energy": jnp.clip(jax.random.uniform(key_list[3], (IJ,), jnp.float32, -2.5, -0.5), -2.5, -0.5),
        "vir_energy": jnp.clip(jax.random.uniform(key_list[4], (NIRREP, NB), jnp.float32, 0.5, 6.0), 0.5, 6.0),
    }


def grouped(amplitudes, ladder_ints, group_sizes):
    nrows = amplitudes.shape[0]
    width = ladder_ints.shape[2]
    ends = jnp.cumsum(group_sizes).astype(jnp.int32)
    starts = (ends - group_sizes).astype(jnp.int32)
    total = jnp.zeros((nrows, width), jnp.float32)
    for irrep in range(NIRREP):
        first = starts[irrep]
        count = group_sizes[irrep].astype(jnp.int32)
        blocks = ((count + BLOCK - 1) // BLOCK).astype(jnp.int32)
        table = ladder_ints[irrep]

        def step(index, acc, first=first, count=count, table=table):
            nominal = (first + index * BLOCK).astype(jnp.int32)
            begin = jnp.minimum(nominal, nrows - BLOCK).astype(jnp.int32)
            rows = lax.dynamic_slice_in_dim(amplitudes, begin, BLOCK, 0)
            ids = begin + jnp.arange(BLOCK, dtype=jnp.int32)
            keep = (ids >= nominal) & (ids < first + count)
            prod = jnp.dot(rows, table, preferred_element_type=jnp.float32)
            prod = jnp.where(keep[:, None], prod, jnp.zeros_like(prod))
            current = lax.dynamic_slice_in_dim(acc, begin, BLOCK, 0)
            return lax.dynamic_update_slice_in_dim(acc, current + prod, begin, 0)

        total = lax.fori_loop(0, blocks, step, total)
    return total


def reference(ladder_ints, amplitudes, group_sizes, occ_energy, vir_energy):
    ladder = grouped(amplitudes, ladder_ints, group_sizes)
    ends = jnp.cumsum(group_sizes).astype(jnp.int32)
    row_ids = jnp.arange(IJ, dtype=jnp.int32)
    irreps = jnp.sum((row_ids[:, None] >= ends[None, :]).astype(jnp.int32), axis=1).astype(jnp.int32)
    denom = occ_energy[:, None] - vir_energy[irreps]
    return (ladder / denom).astype(jnp.bfloat16)
```

```python
import functools

import jax
import jax.numpy as jnp
from jax import lax
from jax.experimental import pallas as pl
from jax.experimental.pallas import tpu as pltpu
from jax.sharding import PartitionSpec as P

NIRREP = 8
NX, NZ, NC = 4, 8, 2
UNIT = 48
TILE = 128
WIDE = 384
PEAK = 32700.0
STEPS = 128.0
ROUND = 12582912.0
LEAST = 2.0**-100


def permutation(dx, dz, dc):
    def at(x, z, c):
        return ((x % NX) * NZ + z % NZ) * NC + c % NC

    return [
        (at(x, z, c), at(x + dx, z + dz, c + dc))
        for x in range(NX)
        for z in range(NZ)
        for c in range(NC)
    ]


def shifted(value, dx, dz, dc):
    return lax.ppermute(value, "cd", permutation(dx, dz, dc))


def ladder_kernel(offset, meta, sizes, t0_ref, t1_ref, v0_ref, v1_ref, out_ref, acc_ref):
    rows = acc_ref.shape[0]
    base = meta[2] * (2 * rows) + offset
    acc_ref[...] = jnp.zeros_like(acc_ref)
    first = jnp.int32(0)
    for g in range(NIRREP):
        last = first + sizes[g]
        low = jnp.clip(first - base, 0, rows)
        high = jnp.clip(last - base, 0, rows)

        def tile(t, carry, g=g, low=low, high=high):
            at = pl.multiple_of(t * TILE, TILE)
            prod = jnp.dot(t0_ref[pl.ds(at, TILE), :], v0_ref[g], preferred_element_type=jnp.float32)
            prod += jnp.dot(t1_ref[pl.ds(at, TILE), :], v1_ref[g], preferred_element_type=jnp.float32)
            ids = at + lax.broadcasted_iota(jnp.int32, prod.shape, 0)
            keep = (ids >= low) & (ids < high)
            acc_ref[pl.ds(at, TILE), :] += jnp.where(keep, prod, 0.0)
            return carry

        begin = low >> 7
        lax.fori_loop(begin, jnp.where(high > low, (high + TILE - 1) >> 7, begin), tile, 0)
        first = last
    for t in range(rows // TILE):
        out_ref[:, t * TILE : (t + 1) * TILE] = acc_ref[t * TILE : (t + 1) * TILE, :].T


def ladder(meta, sizes, t0, t1, v0, v1, offset, rows):
    depth, width = v0.shape[1:]
    part = offset // rows
    spec_t = pl.BlockSpec((rows, depth), lambda i, *_: (part, 0))
    spec_v = pl.BlockSpec((NIRREP, depth, WIDE), lambda i, *_: (0, 0, i))
    return pl.pallas_call(
        functools.partial(ladder_kernel, offset),
        out_shape=jax.ShapeDtypeStruct((width, rows), jnp.float32),
        grid_spec=pltpu.PrefetchScalarGridSpec(
            num_scalar_prefetch=2,
            grid=(width // WIDE,),
            in_specs=[spec_t, spec_t, spec_v, spec_v],
            out_specs=pl.BlockSpec((WIDE, rows), lambda i, *_: (i, 0)),
            scratch_shapes=[pltpu.VMEM((rows, WIDE), jnp.float32)],
        ),
        compiler_params=pltpu.CompilerParams(vmem_limit_bytes=40 << 20),
        cost_estimate=pl.CostEstimate(
            flops=4 * rows * depth * width * 2, bytes_accessed=30 << 20, transcendentals=0
        ),
        name="ladder",
    )(meta, sizes, t0, t1, v0, v1)


def scale_of(code):
    return jnp.exp2(code * (1.0 / STEPS)) * (1.0 / PEAK)


def decode_scales(message_ref, scales_ref):
    n = message_ref.shape[0] // UNIT
    scales_ref[...] = scale_of(message_ref[n * UNIT : n * UNIT + 16, :].astype(jnp.float32))


def received(message_ref, scales_ref, unit):
    at = jnp.maximum(unit, 0)
    factor = jnp.where(unit >= 0, 1.0, 0.0)
    values = message_ref[pl.ds(pl.multiple_of(at * UNIT, 16), UNIT), :].astype(jnp.float32)
    return values * (scales_ref[pl.ds(at, 1), :] * factor)


def hop_kernel(n, group, units, n_msgs, meta, *refs):
    own_refs, refs = refs[:2], refs[2:]
    msg_refs, refs = refs[:n_msgs], refs[n_msgs:]
    out_refs, refs = refs[:2], refs[2:]
    code_refs, scale_refs = refs[:2], refs[2:]
    step = pl.program_id(0)

    @pl.when(step == 0)
    def _():
        for m, s in zip(msg_refs, scale_refs):
            decode_scales(m, s)
        for c in code_refs:
            c[...] = jnp.zeros_like(c)

    for d in range(2):
        for k in range(group):
            i = step * group + k
            value = own_refs[d][k * UNIT : (k + 1) * UNIT, :]
            for j, unit in units(d, i, meta):
                value = value + received(msg_refs[j], scale_refs[j], unit)
            most = jnp.maximum(jnp.max(jnp.abs(value), axis=0, keepdims=True), LEAST)
            code = jnp.floor(jnp.log2(most) * STEPS) + 2.0
            coded = value * (1.0 / scale_of(code))
            coded = (coded + ROUND) - ROUND
            rows = pl.ds(pl.multiple_of(i * UNIT, 16), UNIT)
            out_refs[d][rows, :] = coded.astype(jnp.int32).astype(jnp.int16)
            code_refs[d][pl.ds(i, 1), :] = code

    @pl.when(step == n // group - 1)
    def _():
        for d in range(2):
            codes = code_refs[d][...].astype(jnp.int32).astype(jnp.int16)
            out_refs[d][n * UNIT : n * UNIT + 16, :] = codes


def hop(meta, own, msgs, n, group, block, units):
    rows = own.shape[1]

    def own_spec(d):
        return pl.BlockSpec((group * UNIT, rows), lambda s, meta: (block(d, s, meta), 0))

    def whole(shape):
        return pl.BlockSpec(shape, lambda s, meta: (0, 0))

    shape = (n * UNIT + 16, rows)
    return pl.pallas_call(
        functools.partial(hop_kernel, n, group, units, len(msgs)),
        out_shape=[jax.ShapeDtypeStruct(shape, jnp.int16)] * 2,
        grid_spec=pltpu.PrefetchScalarGridSpec(
            num_scalar_prefetch=1,
            grid=(n // group,),
            in_specs=[own_spec(0), own_spec(1)] + [whole(m.shape) for m in msgs],
            out_specs=[whole(shape)] * 2,
            scratch_shapes=[pltpu.VMEM((16, rows), jnp.float32)] * (2 + len(msgs)),
        ),
        compiler_params=pltpu.CompilerParams(vmem_limit_bytes=40 << 20),
        cost_estimate=pl.CostEstimate(
            flops=20 * n * UNIT * rows, bytes_accessed=16 * n * UNIT * rows, transcendentals=0
        ),
        name="hop",
    )(meta, own, own, *msgs)


def both_ways(pair, axis):
    dx, dz = (1, 0) if axis == "x" else (0, 1)
    return [shifted(pair[0], dx, dz, 0), shifted(pair[1], -dx, -dz, 0)]


def ring(meta, own, before, axis, count, unit_of, block_of):
    size, here = (NX, 0) if axis == "x" else (NZ, 1)
    sign = (1, -1)
    kept = len(before)
    moving = []
    for step in range(size // 2):
        ahead = size // 2 - step
        halved = step == 0
        n = count // 2 if halved else count
        group = min(4 if count == 16 else 2, n)

        def place(d, meta, ahead=ahead):
            return (meta[here] + sign[d] * ahead + size) & (size - 1)

        def block(d, s, meta, group=group, halved=halved, place=place):
            skip = d * (count // 2 // group) if halved else 0
            return block_of(place(d, meta), group, s + skip, meta)

        def units(d, i, meta, step=step, halved=halved, place=place):
            at = i + d * (count // 2) if halved else i
            found = [(j, unit_of(place(d, meta), at)) for j in range(kept)]
            if step == 1:
                half = count // 2
                found.append((kept + d, jnp.where(i < half, i, -1) if d == 0 else jnp.where(i >= half, i - half, -1)))
            elif step > 1:
                found.append((kept + d, i))
            return found

        moving = both_ways(hop(meta, own, before + moving, n, group, block, units), axis)
    return moving


def last_kernel(n_parts, meta, sizes, *refs):
    own_refs, refs = refs[:n_parts], refs[n_parts:]
    msg_refs, refs = refs[: 4 * n_parts], refs[4 * n_parts :]
    occ_ref, vir_ref, mine_ref, other_ref = refs[:4]
    scale_refs = refs[4:]
    x, z, core = meta[0], meta[1], meta[2]
    rows = own_refs[0].shape[1]
    for m, s in zip(msg_refs, scale_refs):
        decode_scales(m, s)
    for p in range(n_parts):
        ids = core * (n_parts * rows) + p * rows + lax.broadcasted_iota(jnp.int32, (1, rows), 1)
        for out_ref, c in ((mine_ref, core), (other_ref, 1 - core)):
            at = pl.ds(pl.multiple_of(c * UNIT, 16), UNIT)
            total = own_refs[p][at, :]
            before = (2 * z if p == 0 else 2 * x) + c
            for j, unit in enumerate((before, before, c, c)):
                total = total + received(msg_refs[4 * p + j], scale_refs[4 * p + j], unit)
            vir = jnp.zeros((UNIT, rows), jnp.float32)
            first = jnp.int32(0)
            for g in range(NIRREP):
                last = first + sizes[g]
                inside = jnp.where((ids >= first) & (ids < last), 1.0, 0.0)
                vir = vir + inside * vir_ref[at, g : g + 1]
                first = last
            cols = slice(p * rows, (p + 1) * rows)
            out_ref[:, cols] = (total / (occ_ref[:, cols] - vir)).astype(jnp.bfloat16)


def last(meta, sizes, owns, msgs, occ, vir):
    rows = owns[0].shape[1]

    def whole(shape):
        return pl.BlockSpec(shape, lambda s, meta, sizes: (0, 0))

    own_spec = pl.BlockSpec((2 * UNIT, rows), lambda s, meta, sizes: (meta[0] * NZ + meta[1], 0))
    shape = (UNIT, len(owns) * rows)
    return pl.pallas_call(
        functools.partial(last_kernel, len(owns)),
        out_shape=[jax.ShapeDtypeStruct(shape, jnp.bfloat16)] * 2,
        grid_spec=pltpu.PrefetchScalarGridSpec(
            num_scalar_prefetch=2,
            grid=(1,),
            in_specs=[own_spec] * len(owns) + [whole(m.shape) for m in msgs] + [whole(occ.shape), whole(vir.shape)],
            out_specs=[whole(shape)] * 2,
            scratch_shapes=[pltpu.VMEM((16, rows), jnp.float32)] * len(msgs),
        ),
        compiler_params=pltpu.CompilerParams(vmem_limit_bytes=40 << 20),
        name="last",
    )(meta, sizes, *owns, *msgs, occ, vir)


def body(ladder_ints, amplitudes, group_sizes, occ_energy, vir_energy):
    place = lax.axis_index("cd").astype(jnp.int32)
    x, z, core = place // (NZ * NC), (place // NC) % NZ, place % NC
    meta = jnp.stack([x, z, core]).astype(jnp.int32)
    their_ints = shifted(ladder_ints, 0, 0, 1)
    slab = lax.all_gather(amplitudes, "ab", axis=0, tiled=True)
    half = slab.shape[0] // 2
    my_rows = lax.dynamic_slice_in_dim(slab, core * half, half, 0)
    their_rows = lax.dynamic_slice_in_dim(slab, (1 - core) * half, half, 0)
    got_rows = shifted(their_rows, 0, 0, 1)
    rows = half // 2

    def product(offset):
        return ladder(meta, group_sizes, my_rows, got_rows, ladder_ints, their_ints, offset, rows)

    own_a = product(0)
    own_b = product(rows)

    def block_ax(p, group, s, meta):
        return p * (2 * NZ // group) + s

    def block_az(p, group, s, meta):
        return (meta[0] * NZ + p) * (2 // group) + s

    def block_bz(p, group, s, meta):
        return s * NZ + p

    def block_bx(p, group, s, meta):
        return (p * NZ + meta[1]) * (2 // group) + s

    def next_unit(p, i):
        return 2 * p + i

    ax = ring(meta, own_a, [], "x", 2 * NZ, None, block_ax)
    bz = ring(meta, own_b, [], "z", 2 * NX, None, block_bz)
    az = ring(meta, own_a, ax, "z", 2, next_unit, block_az)
    bx = ring(meta, own_b, bz, "x", 2, next_unit, block_bx)

    owner = lax.axis_index("ab") * ladder_ints.shape[2] + (place // NC) * (2 * UNIT)
    vir = lax.dynamic_slice_in_dim(vir_energy, owner, 2 * UNIT, 1).T
    occ = lax.dynamic_slice_in_dim(occ_energy, core * half, half, 0)[None, :]
    mine, other = last(meta, group_sizes, [own_a, own_b], ax + az + bz + bx, occ, vir)
    got = shifted(other, 0, 0, 1)
    low = jnp.where(core == 0, mine, got)
    high = jnp.where(core == 0, got, mine)
    return jnp.concatenate([low, high], axis=1).T


def solution(mesh):
    placed = (P(None, "cd", "ab"), P("ab", "cd"), P(), P(), P())
    return jax.shard_map(
        body, mesh=mesh, in_specs=placed, out_specs=P(None, ("ab", "cd")), check_vma=False
    )
```

```python
import functools

import jax
import jax.numpy as jnp
from jax import lax
from jax.experimental import pallas as pl
from jax.experimental.pallas import tpu as pltpu
from jax.sharding import PartitionSpec as P

NIRREP = 8
NX, NZ, NC = 4, 8, 2
UNIT = 48
WIDE = 256
LADDER_VMEM = 42 << 20
HOP_VMEM = 20 << 20
PEAK = 32700.0
STEPS = 128.0
ROUND = 12582912.0
LEAST = 2.0**-100


def permutation(dx, dz, dc):
    def at(x, z, c):
        return ((x % NX) * NZ + z % NZ) * NC + c % NC

    return [
        (at(x, z, c), at(x + dx, z + dz, c + dc))
        for x in range(NX)
        for z in range(NZ)
        for c in range(NC)
    ]


def shifted(value, dx, dz, dc):
    return lax.ppermute(value, "cd", permutation(dx, dz, dc))


def span(meta, sizes, start, rows):
    end, low, high = jnp.int32(0), jnp.int32(0), jnp.int32(0)
    for g in range(NIRREP - 1):
        end = end + sizes[g]
        low = low + (end <= start).astype(jnp.int32)
        high = high + (end < start + rows).astype(jnp.int32)
    return low, high


def ladder_kernel(part, meta, sizes, t0_ref, t1_ref, v0_ref, v1_ref, out_ref, kept_ref, total_ref, sem, kept_sem):
    width, rows = total_ref.shape
    g = pl.program_id(0)
    first = jnp.int32(0)
    for k in range(NIRREP - 1):
        first = first + jnp.where(k < g, sizes[k], 0)
    last = first + sizes[g]
    base = meta[2] * (2 * rows) + part * rows
    pieces = [slice(j * WIDE, (j + 1) * WIDE) for j in range(width // WIDE)]

    def product(piece):
        table = jnp.concatenate([v0_ref[0, :, piece], v1_ref[0, :, piece]], axis=0)
        slab = jnp.concatenate([t0_ref[0], t1_ref[0]], axis=0)
        return lax.dot_general(table, slab, (((0,), (0,)), ((), ())), preferred_element_type=jnp.float32)

    def copy(piece):
        return pltpu.make_async_copy(total_ref.at[piece], out_ref.at[piece], sem)

    @pl.when((first <= base) & (last > base))
    def _():
        for piece in pieces:
            total_ref[piece, :] = product(piece)

            @pl.when(last >= base + rows)
            def _(piece=piece):
                copy(piece).start()

    @pl.when((first > base) & (first < base + rows) & (last > first))
    def _():
        ids = base + lax.broadcasted_iota(jnp.int32, (1, rows), 1)
        for piece in pieces:
            total_ref[piece, :] = jnp.where(ids >= first, product(piece), total_ref[piece, :])

            @pl.when(last >= base + rows)
            def _(piece=piece):
                copy(piece).start()

    @pl.when(g == NIRREP - 1)
    def _():
        count = 1 if part == 0 else NX
        size = kept_ref.shape[0] // count
        copies = []
        for k in range(count):
            source = meta[0] * size if part == 0 else (k * NZ + meta[1]) * size
            rows_from = pl.ds(pl.multiple_of(source, 2 * UNIT), size)
            copies.append(
                pltpu.make_async_copy(total_ref.at[rows_from], kept_ref.at[pl.ds(k * size, size)], kept_sem.at[k])
            )
        for c in copies:
            c.start()
        for piece in pieces:
            copy(piece).wait()
        for c in copies:
            c.wait()


def ladder(part, meta, sizes, t0, t1, v0, v1):
    depth, width = v0.shape[1:]
    rows = t0.shape[2]
    kept = width // (NX if part == 0 else NZ)

    def table(g, meta, sizes):
        low, high = span(meta, sizes, meta[2] * (2 * rows) + part * rows, rows)
        return jnp.minimum(jnp.maximum(g, low), high), 0, 0

    spec_t = pl.BlockSpec((1, depth, rows), lambda g, *_: (part, 0, 0))
    spec_v = pl.BlockSpec((1, depth, width), table)
    return pl.pallas_call(
        functools.partial(ladder_kernel, part),
        out_shape=[jax.ShapeDtypeStruct((n, rows), jnp.float32) for n in (width, kept)],
        grid_spec=pltpu.PrefetchScalarGridSpec(
            num_scalar_prefetch=2,
            grid=(NIRREP,),
            in_specs=[spec_t, spec_t, spec_v, spec_v],
            out_specs=[pl.BlockSpec(memory_space=pl.ANY)] * 2,
            scratch_shapes=[
                pltpu.VMEM((width, rows), jnp.float32),
                pltpu.SemaphoreType.DMA,
                pltpu.SemaphoreType.DMA((NX,)),
            ],
        ),
        compiler_params=pltpu.CompilerParams(vmem_limit_bytes=LADDER_VMEM),
        cost_estimate=pl.CostEstimate(
            flops=8 * rows * depth * width, bytes_accessed=30 << 20, transcendentals=0
        ),
        name="ladder",
    )(meta, sizes, t0, t1, v0, v1)


def scale_of(code):
    return jnp.exp2(code * (1.0 / STEPS)) * (1.0 / PEAK)


def decode_scales(message_ref, scales_ref):
    n = message_ref.shape[0] // UNIT
    scales_ref[...] = scale_of(message_ref[n * UNIT : n * UNIT + 16, :].astype(jnp.float32))


def received(message_ref, scales_ref, unit):
    at = jnp.maximum(unit, 0)
    factor = jnp.where(unit >= 0, 1.0, 0.0)
    values = message_ref[pl.ds(pl.multiple_of(at * UNIT, 16), UNIT), :].astype(jnp.float32)
    return values * (scales_ref[pl.ds(at, 1), :] * factor)


def encoded(value):
    most = jnp.maximum(jnp.max(jnp.abs(value), axis=0, keepdims=True), LEAST)
    code = jnp.floor(jnp.log2(most) * STEPS) + 2.0
    coded = value * (1.0 / scale_of(code))
    coded = (coded + ROUND) - ROUND
    return coded.astype(jnp.int32).astype(jnp.int16), code


def hop_kernel(n, group, units, n_msgs, meta, *refs):
    own_refs, refs = refs[:2], refs[2:]
    msg_refs, refs = refs[:n_msgs], refs[n_msgs:]
    out_refs, refs = refs[:2], refs[2:]
    code_refs, scale_refs = refs[:2], refs[2:]
    step = pl.program_id(0)

    @pl.when(step == 0)
    def _():
        for m, s in zip(msg_refs, scale_refs):
            decode_scales(m, s)
        for c in code_refs:
            c[...] = jnp.zeros_like(c)

    for d in range(2):
        for k in range(group):
            i = step * group + k
            value = own_refs[d][k * UNIT : (k + 1) * UNIT, :]
            for j, unit in units(d, i, meta):
                value = value + received(msg_refs[j], scale_refs[j], unit)
            coded, code = encoded(value)
            rows = pl.ds(pl.multiple_of(i * UNIT, 16), UNIT)
            out_refs[d][rows, :] = coded
            code_refs[d][pl.ds(i, 1), :] = code

    @pl.when(step == n // group - 1)
    def _():
        for d in range(2):
            codes = code_refs[d][...].astype(jnp.int32).astype(jnp.int16)
            out_refs[d][n * UNIT : n * UNIT + 16, :] = codes


def hop(meta, own, msgs, n, group, block, units):
    rows = own.shape[1]

    def own_spec(d):
        return pl.BlockSpec((group * UNIT, rows), lambda s, meta: (block(d, s, meta), 0))

    def whole(shape):
        return pl.BlockSpec(shape, lambda s, meta: (0, 0))

    shape = (n * UNIT + 16, rows)
    return pl.pallas_call(
        functools.partial(hop_kernel, n, group, units, len(msgs)),
        out_shape=[jax.ShapeDtypeStruct(shape, jnp.int16)] * 2,
        grid_spec=pltpu.PrefetchScalarGridSpec(
            num_scalar_prefetch=1,
            grid=(n // group,),
            in_specs=[own_spec(0), own_spec(1)] + [whole(m.shape) for m in msgs],
            out_specs=[whole(shape)] * 2,
            scratch_shapes=[pltpu.VMEM((16, rows), jnp.float32)] * (2 + len(msgs)),
        ),
        compiler_params=pltpu.CompilerParams(vmem_limit_bytes=HOP_VMEM),
        cost_estimate=pl.CostEstimate(
            flops=20 * n * UNIT * rows, bytes_accessed=16 * n * UNIT * rows, transcendentals=0
        ),
        name="hop",
    )(meta, own, own, *msgs)


def both_ways(pair, axis):
    dx, dz = (1, 0) if axis == "x" else (0, 1)
    return [shifted(pair[0], dx, dz, 0), shifted(pair[1], -dx, -dz, 0)]


def ring(meta, own, axis, count, block_of):
    size, here = (NX, 0) if axis == "x" else (NZ, 1)
    sign = (1, -1)
    moving = []
    for step in range(size // 2):
        ahead = size // 2 - step
        halved = step == 0
        n = count // 2 if halved else count
        group = 4 if count == 16 else 2

        def place(d, meta, ahead=ahead):
            return (meta[here] + sign[d] * ahead + size) & (size - 1)

        def block(d, s, meta, group=group, halved=halved, place=place):
            skip = d * (count // 2 // group) if halved else 0
            return block_of(place(d, meta), group, s + skip, meta)

        def units(d, i, meta, step=step):
            if step == 0:
                return []
            if step > 1:
                return [(d, i)]
            half = count // 2
            return [(d, jnp.where(i < half, i, -1) if d == 0 else jnp.where(i >= half, i - half, -1))]

        moving = both_ways(hop(meta, own, moving, n, group, block, units), axis)
    return moving


def spread_kernel(size, here, meta, own_ref, *refs):
    msg_refs, out_refs, (code_ref, *scale_refs) = refs[:2], refs[2 : size + 1], refs[size + 1 :]
    for m, s in zip(msg_refs, scale_refs):
        decode_scales(m, s)
    code_ref[...] = jnp.zeros_like(code_ref)
    for d, out_ref in enumerate(out_refs):
        place = (meta[here] + d + 1) & (size - 1)
        for k in range(2):
            unit = 2 * place + k
            value = own_ref[pl.ds(pl.multiple_of(unit * UNIT, 16), UNIT), :]
            for m, s in zip(msg_refs, scale_refs):
                value = value + received(m, s, unit)
            out_ref[k * UNIT : (k + 1) * UNIT, :], code_ref[k : k + 1, :] = encoded(value)
        out_ref[2 * UNIT :, :] = code_ref[...].astype(jnp.int32).astype(jnp.int16)


def spread(meta, own, msgs, axis):
    size, here = (NX, 0) if axis == "x" else (NZ, 1)
    rows = own.shape[1]
    shape = (2 * UNIT + 16, rows)

    def whole(shape):
        return pl.BlockSpec(shape, lambda s, meta: (0, 0))

    out = pl.pallas_call(
        functools.partial(spread_kernel, size, here),
        out_shape=[jax.ShapeDtypeStruct(shape, jnp.int16)] * (size - 1),
        grid_spec=pltpu.PrefetchScalarGridSpec(
            num_scalar_prefetch=1,
            grid=(1,),
            in_specs=[whole(a.shape) for a in (own, *msgs)],
            out_specs=[whole(shape)] * (size - 1),
            scratch_shapes=[pltpu.VMEM((16, rows), jnp.float32)] * 3,
        ),
        compiler_params=pltpu.CompilerParams(vmem_limit_bytes=HOP_VMEM),
        name="spread",
    )(meta, own, *msgs)
    return [shifted(m, *((d + 1, 0) if axis == "x" else (0, d + 1)), 0) for d, m in enumerate(out)]


def last_kernel(n_parts, meta, sizes, *refs):
    own_refs, refs = refs[:n_parts], refs[n_parts:]
    n_msgs = (len(refs) - 4) // 2
    msg_refs, refs = refs[:n_msgs], refs[n_msgs:]
    parts = (NZ + 1, NX + 1)
    occ_ref, vir_ref, mine_ref, other_ref = refs[:4]
    scale_refs = refs[4:]
    x, z, core = meta[0], meta[1], meta[2]
    rows = own_refs[0].shape[1]
    for m, s in zip(msg_refs, scale_refs):
        decode_scales(m, s)
    for p in range(n_parts):
        ids = core * (n_parts * rows) + p * rows + lax.broadcasted_iota(jnp.int32, (1, rows), 1)
        for out_ref, c in ((mine_ref, core), (other_ref, 1 - core)):
            at = pl.ds(pl.multiple_of(c * UNIT, 16), UNIT)
            total = own_refs[p][at, :]
            before = (2 * z if p == 0 else 2 * x) + c
            for j in range(parts[p]):
                at_msg = sum(parts[:p]) + j
                total = total + received(msg_refs[at_msg], scale_refs[at_msg], before if j < 2 else c)
            vir = jnp.zeros((UNIT, rows), jnp.float32)
            first = jnp.int32(0)
            for g in range(NIRREP):
                last = first + sizes[g]
                inside = jnp.where((ids >= first) & (ids < last), 1.0, 0.0)
                vir = vir + inside * vir_ref[at, g : g + 1]
                first = last
            cols = slice(p * rows, (p + 1) * rows)
            out_ref[:, cols] = (total / (occ_ref[:, cols] - vir)).astype(jnp.bfloat16)


def last(meta, sizes, owns, msgs, occ, vir):
    rows = owns[0].shape[1]

    def whole(shape):
        return pl.BlockSpec(shape, lambda s, meta, sizes: (0, 0))

    own_specs = [
        pl.BlockSpec((2 * UNIT, rows), lambda s, meta, sizes, axis=axis: (meta[axis], 0)) for axis in (1, 0)
    ]
    shape = (UNIT, len(owns) * rows)
    return pl.pallas_call(
        functools.partial(last_kernel, len(owns)),
        out_shape=[jax.ShapeDtypeStruct(shape, jnp.bfloat16)] * 2,
        grid_spec=pltpu.PrefetchScalarGridSpec(
            num_scalar_prefetch=2,
            grid=(1,),
            in_specs=own_specs + [whole(m.shape) for m in msgs] + [whole(occ.shape), whole(vir.shape)],
            out_specs=[whole(shape)] * 2,
            scratch_shapes=[pltpu.VMEM((16, rows), jnp.float32)] * len(msgs),
        ),
        compiler_params=pltpu.CompilerParams(vmem_limit_bytes=HOP_VMEM),
        name="last",
    )(meta, sizes, *owns, *msgs, occ, vir)


def body(ladder_ints, amplitudes, group_sizes, occ_energy, vir_energy):
    place = lax.axis_index("cd").astype(jnp.int32)
    x, z, core = place // (NZ * NC), (place // NC) % NZ, place % NC
    meta = jnp.stack([x, z, core]).astype(jnp.int32)
    their_ints = shifted(ladder_ints, 0, 0, 1)
    slab = lax.all_gather(amplitudes.T, "ab", axis=0)
    parts, _, rows = slab.shape
    parts = parts // NC
    my_rows = lax.dynamic_slice_in_dim(slab, core * parts, parts, 0)
    their_rows = lax.dynamic_slice_in_dim(slab, (1 - core) * parts, parts, 0)
    got_rows = shifted(their_rows, 0, 0, 1)
    half = parts * rows
    operands = (meta, group_sizes, my_rows, got_rows, ladder_ints, their_ints)
    (own_a, kept_a), (own_b, kept_b) = ladder(0, *operands), ladder(1, *operands)

    def block_ax(p, group, s, meta):
        return p * (2 * NZ // group) + s

    def block_bz(p, group, s, meta):
        return s * NZ + p

    ax = ring(meta, own_a, "x", 2 * NZ, block_ax)
    bz = ring(meta, own_b, "z", 2 * NX, block_bz)
    chunk = place // NC * (2 * UNIT)
    owner = lax.axis_index("ab") * ladder_ints.shape[2] + chunk
    vir = lax.dynamic_slice_in_dim(vir_energy, owner, 2 * UNIT, 1).T
    occ = lax.dynamic_slice_in_dim(occ_energy, core * half, half, 0)[None, :]
    *ax, vir, occ = lax.optimization_barrier((*ax, vir, occ))
    az = spread(meta, kept_a, ax, "z")
    bx = spread(meta, kept_b, bz, "x")
    mine, other = last(meta, group_sizes, [kept_a, kept_b], ax + az + bz + bx, occ, vir)
    got = shifted(other, 0, 0, 1)
    low = jnp.where(core == 0, mine, got)
    high = jnp.where(core == 0, got, mine)
    return jnp.concatenate([low, high], axis=1).T


def solution(mesh):
    placed = (P(None, "cd", "ab"), P("ab", "cd"), P(), P(), P())
    return jax.shard_map(
        body, mesh=mesh, in_specs=placed, out_specs=P(None, ("ab", "cd")), check_vma=False
    )
```

```python
import functools

import jax
import jax.numpy as jnp
from jax import lax
from jax.experimental import pallas as pl
from jax.experimental.pallas import tpu as pltpu
from jax.sharding import PartitionSpec as P

NIRREP = 8
NX, NZ, NC = 4, 8, 2
UNIT = 48
WIDE = 256
TILE = 256
LADDER_VMEM = 42 << 20
HOP_VMEM = 20 << 20
PEAK = 32700.0
STEPS = 128.0
ROUND = 12582912.0
LEAST = 2.0**-100


def permutation(dx, dz, dc):
    def at(x, z, c):
        return ((x % NX) * NZ + z % NZ) * NC + c % NC

    return [
        (at(x, z, c), at(x + dx, z + dz, c + dc))
        for x in range(NX)
        for z in range(NZ)
        for c in range(NC)
    ]


def shifted(value, dx, dz, dc):
    return lax.ppermute(value, "cd", permutation(dx, dz, dc))


def span(meta, sizes, start, rows):
    end, low, high = jnp.int32(0), jnp.int32(0), jnp.int32(0)
    for g in range(NIRREP - 1):
        end = end + sizes[g]
        low = low + (end <= start).astype(jnp.int32)
        high = high + (end < start + rows).astype(jnp.int32)
    return low, high


def ladder_kernel(part, meta, sizes, t0_ref, t1_ref, v0_ref, v1_ref, out_ref, kept_ref, total_ref, sem, kept_sem):
    width, rows = total_ref.shape
    g = pl.program_id(0)
    first = jnp.int32(0)
    for k in range(NIRREP - 1):
        first = first + jnp.where(k < g, sizes[k], 0)
    last = first + sizes[g]
    base = meta[2] * (2 * rows) + part * rows
    pieces = [slice(j * WIDE, (j + 1) * WIDE) for j in range(width // WIDE)]
    tiles = [slice(q * TILE, (q + 1) * TILE) for q in range(rows // TILE)]

    def copy(q):
        return pltpu.make_async_copy(total_ref.at[:, tiles[q]], out_ref.at[:, tiles[q]], sem.at[q])

    for q, tile in enumerate(tiles):
        begin = base + q * TILE
        slab = (0, slice(None), tile)

        def product(piece, slab=slab):
            table = jnp.concatenate([v0_ref[0, :, piece], v1_ref[0, :, piece]], axis=0)
            both = jnp.concatenate([t0_ref[slab], t1_ref[slab]], axis=0)
            return lax.dot_general(table, both, (((0,), (0,)), ((), ())), preferred_element_type=jnp.float32)

        @pl.when((first <= begin) & (last > begin))
        def _(tile=tile, product=product):
            for piece in pieces:
                total_ref[piece, tile] = product(piece)

        @pl.when((first > begin) & (first < begin + TILE) & (last > first))
        def _(tile=tile, product=product, begin=begin):
            ids = begin + lax.broadcasted_iota(jnp.int32, (1, TILE), 1)
            for piece in pieces:
                total_ref[piece, tile] = jnp.where(ids >= first, product(piece), total_ref[piece, tile])

        @pl.when((first < begin + TILE) & (last >= begin + TILE))
        def _(q=q):
            copy(q).start()

    @pl.when(g == NIRREP - 1)
    def _():
        count = 1 if part == 0 else NX
        size = kept_ref.shape[0] // count
        copies = []
        for k in range(count):
            source = meta[0] * size if part == 0 else (k * NZ + meta[1]) * size
            rows_from = pl.ds(pl.multiple_of(source, 2 * UNIT), size)
            copies.append(
                pltpu.make_async_copy(total_ref.at[rows_from], kept_ref.at[pl.ds(k * size, size)], kept_sem.at[k])
            )
        for c in copies:
            c.start()
        for q in range(len(tiles)):
            copy(q).wait()
        for c in copies:
            c.wait()


def ladder(part, meta, sizes, t0, t1, v0, v1):
    depth, width = v0.shape[1:]
    rows = t0.shape[2]
    kept = width // (NX if part == 0 else NZ)

    def table(g, meta, sizes):
        low, high = span(meta, sizes, meta[2] * (2 * rows) + part * rows, rows)
        return jnp.minimum(jnp.maximum(g, low), high), 0, 0

    spec_t = pl.BlockSpec((1, depth, rows), lambda g, *_: (part, 0, 0))
    spec_v = pl.BlockSpec((1, depth, width), table)
    return pl.pallas_call(
        functools.partial(ladder_kernel, part),
        out_shape=[jax.ShapeDtypeStruct((n, rows), jnp.float32) for n in (width, kept)],
        grid_spec=pltpu.PrefetchScalarGridSpec(
            num_scalar_prefetch=2,
            grid=(NIRREP,),
            in_specs=[spec_t, spec_t, spec_v, spec_v],
            out_specs=[pl.BlockSpec(memory_space=pl.ANY)] * 2,
            scratch_shapes=[
                pltpu.VMEM((width, rows), jnp.float32),
                pltpu.SemaphoreType.DMA((rows // TILE,)),
                pltpu.SemaphoreType.DMA((NX,)),
            ],
        ),
        compiler_params=pltpu.CompilerParams(vmem_limit_bytes=LADDER_VMEM),
        cost_estimate=pl.CostEstimate(
            flops=8 * rows * depth * width, bytes_accessed=30 << 20, transcendentals=0
        ),
        name="ladder",
    )(meta, sizes, t0, t1, v0, v1)


def scale_of(code):
    return jnp.exp2(code * (1.0 / STEPS)) * (1.0 / PEAK)


def decode_scales(message_ref, scales_ref):
    n = message_ref.shape[0] // UNIT
    scales_ref[...] = scale_of(message_ref[n * UNIT : n * UNIT + 16, :].astype(jnp.float32))


def received(message_ref, scales_ref, unit):
    at = jnp.maximum(unit, 0)
    factor = jnp.where(unit >= 0, 1.0, 0.0)
    values = message_ref[pl.ds(pl.multiple_of(at * UNIT, 16), UNIT), :].astype(jnp.float32)
    return values * (scales_ref[pl.ds(at, 1), :] * factor)


def encoded(value):
    most = jnp.maximum(jnp.max(jnp.abs(value), axis=0, keepdims=True), LEAST)
    code = jnp.floor(jnp.log2(most) * STEPS) + 2.0
    coded = value * (1.0 / scale_of(code))
    coded = (coded + ROUND) - ROUND
    return coded.astype(jnp.int32).astype(jnp.int16), code


def hop_kernel(n, group, units, n_msgs, meta, *refs):
    own_refs, refs = refs[:2], refs[2:]
    msg_refs, refs = refs[:n_msgs], refs[n_msgs:]
    out_refs, refs = refs[:2], refs[2:]
    code_refs, scale_refs = refs[:2], refs[2:]
    step = pl.program_id(0)

    @pl.when(step == 0)
    def _():
        for m, s in zip(msg_refs, scale_refs):
            decode_scales(m, s)
        for c in code_refs:
            c[...] = jnp.zeros_like(c)

    for d in range(2):
        for k in range(group):
            i = step * group + k
            value = own_refs[d][k * UNIT : (k + 1) * UNIT, :]
            for j, unit in units(d, i, meta):
                value = value + received(msg_refs[j], scale_refs[j], unit)
            coded, code = encoded(value)
            rows = pl.ds(pl.multiple_of(i * UNIT, 16), UNIT)
            out_refs[d][rows, :] = coded
            code_refs[d][pl.ds(i, 1), :] = code

    @pl.when(step == n // group - 1)
    def _():
        for d in range(2):
            codes = code_refs[d][...].astype(jnp.int32).astype(jnp.int16)
            out_refs[d][n * UNIT : n * UNIT + 16, :] = codes


def hop(meta, own, msgs, n, group, block, units):
    rows = own.shape[1]

    def own_spec(d):
        return pl.BlockSpec((group * UNIT, rows), lambda s, meta: (block(d, s, meta), 0))

    def whole(shape):
        return pl.BlockSpec(shape, lambda s, meta: (0, 0))

    shape = (n * UNIT + 16, rows)
    return pl.pallas_call(
        functools.partial(hop_kernel, n, group, units, len(msgs)),
        out_shape=[jax.ShapeDtypeStruct(shape, jnp.int16)] * 2,
        grid_spec=pltpu.PrefetchScalarGridSpec(
            num_scalar_prefetch=1,
            grid=(n // group,),
            in_specs=[own_spec(0), own_spec(1)] + [whole(m.shape) for m in msgs],
            out_specs=[whole(shape)] * 2,
            scratch_shapes=[pltpu.VMEM((16, rows), jnp.float32)] * (2 + len(msgs)),
        ),
        compiler_params=pltpu.CompilerParams(vmem_limit_bytes=HOP_VMEM),
        cost_estimate=pl.CostEstimate(
            flops=20 * n * UNIT * rows, bytes_accessed=16 * n * UNIT * rows, transcendentals=0
        ),
        name="hop",
    )(meta, own, own, *msgs)


def both_ways(pair, axis):
    dx, dz = (1, 0) if axis == "x" else (0, 1)
    return [shifted(pair[0], dx, dz, 0), shifted(pair[1], -dx, -dz, 0)]


def ring(meta, own, axis, count, block_of, made=None, after=()):
    size, here = (NX, 0) if axis == "x" else (NZ, 1)
    sign = (1, -1)
    moving = []
    for step in range(size // 2):
        ahead = size // 2 - step
        halved = step == 0
        n = count // 2 if halved else count
        group = 4 if count == 16 else 2

        def place(d, meta, ahead=ahead):
            return (meta[here] + sign[d] * ahead + size) & (size - 1)

        def block(d, s, meta, group=group, halved=halved, place=place):
            skip = d * (count // 2 // group) if halved else 0
            return block_of(place(d, meta), group, s + skip, meta)

        def units(d, i, meta, step=step):
            if step == 0:
                return []
            if step > 1:
                return [(d, i)]
            half = count // 2
            return [(d, jnp.where(i < half, i, -1) if d == 0 else jnp.where(i >= half, i - half, -1))]

        if step == 0 and made is None:
            return hop(meta, own, moving, n, group, block, units)
        if step == 1:
            moving = lax.optimization_barrier((*moving, *after))[:2]
        moving = both_ways(made if step == 0 else hop(meta, own, moving, n, group, block, units), axis)
    return moving


def spread_kernel(size, here, meta, own_ref, *refs):
    msg_refs, out_refs, (code_ref, *scale_refs) = refs[:2], refs[2 : size + 1], refs[size + 1 :]
    for m, s in zip(msg_refs, scale_refs):
        decode_scales(m, s)
    code_ref[...] = jnp.zeros_like(code_ref)
    for d, out_ref in enumerate(out_refs):
        place = (meta[here] + d + 1) & (size - 1)
        for k in range(2):
            unit = 2 * place + k
            value = own_ref[pl.ds(pl.multiple_of(unit * UNIT, 16), UNIT), :]
            for m, s in zip(msg_refs, scale_refs):
                value = value + received(m, s, unit)
            out_ref[k * UNIT : (k + 1) * UNIT, :], code_ref[k : k + 1, :] = encoded(value)
        out_ref[2 * UNIT :, :] = code_ref[...].astype(jnp.int32).astype(jnp.int16)


def spread(meta, own, msgs, axis):
    size, here = (NX, 0) if axis == "x" else (NZ, 1)
    rows = own.shape[1]
    shape = (2 * UNIT + 16, rows)

    def whole(shape):
        return pl.BlockSpec(shape, lambda s, meta: (0, 0))

    out = pl.pallas_call(
        functools.partial(spread_kernel, size, here),
        out_shape=[jax.ShapeDtypeStruct(shape, jnp.int16)] * (size - 1),
        grid_spec=pltpu.PrefetchScalarGridSpec(
            num_scalar_prefetch=1,
            grid=(1,),
            in_specs=[whole(a.shape) for a in (own, *msgs)],
            out_specs=[whole(shape)] * (size - 1),
            scratch_shapes=[pltpu.VMEM((16, rows), jnp.float32)] * 3,
        ),
        compiler_params=pltpu.CompilerParams(vmem_limit_bytes=HOP_VMEM),
        name="spread",
    )(meta, own, *msgs)
    return [shifted(m, *((d + 1, 0) if axis == "x" else (0, d + 1)), 0) for d, m in enumerate(out)]


def last_kernel(n_parts, meta, sizes, *refs):
    own_refs, refs = refs[:n_parts], refs[n_parts:]
    n_msgs = (len(refs) - 4) // 2
    msg_refs, refs = refs[:n_msgs], refs[n_msgs:]
    parts = (NZ + 1, NX + 1)
    occ_ref, vir_ref, mine_ref, other_ref = refs[:4]
    scale_refs = refs[4:]
    x, z, core = meta[0], meta[1], meta[2]
    rows = own_refs[0].shape[1]
    for m, s in zip(msg_refs, scale_refs):
        decode_scales(m, s)
    for p in range(n_parts):
        ids = core * (n_parts * rows) + p * rows + lax.broadcasted_iota(jnp.int32, (1, rows), 1)
        for out_ref, c in ((mine_ref, core), (other_ref, 1 - core)):
            at = pl.ds(pl.multiple_of(c * UNIT, 16), UNIT)
            total = own_refs[p][at, :]
            before = (2 * z if p == 0 else 2 * x) + c
            for j in range(parts[p]):
                at_msg = sum(parts[:p]) + j
                total = total + received(msg_refs[at_msg], scale_refs[at_msg], before if j < 2 else c)
            vir = jnp.zeros((UNIT, rows), jnp.float32)
            first = jnp.int32(0)
            for g in range(NIRREP):
                last = first + sizes[g]
                inside = jnp.where((ids >= first) & (ids < last), 1.0, 0.0)
                vir = vir + inside * vir_ref[at, g : g + 1]
                first = last
            cols = slice(p * rows, (p + 1) * rows)
            out_ref[:, cols] = (total / (occ_ref[:, cols] - vir)).astype(jnp.bfloat16)


def last(meta, sizes, owns, msgs, occ, vir):
    rows = owns[0].shape[1]

    def whole(shape):
        return pl.BlockSpec(shape, lambda s, meta, sizes: (0, 0))

    own_specs = [
        pl.BlockSpec((2 * UNIT, rows), lambda s, meta, sizes, axis=axis: (meta[axis], 0)) for axis in (1, 0)
    ]
    shape = (UNIT, len(owns) * rows)
    return pl.pallas_call(
        functools.partial(last_kernel, len(owns)),
        out_shape=[jax.ShapeDtypeStruct(shape, jnp.bfloat16)] * 2,
        grid_spec=pltpu.PrefetchScalarGridSpec(
            num_scalar_prefetch=2,
            grid=(1,),
            in_specs=own_specs + [whole(m.shape) for m in msgs] + [whole(occ.shape), whole(vir.shape)],
            out_specs=[whole(shape)] * 2,
            scratch_shapes=[pltpu.VMEM((16, rows), jnp.float32)] * len(msgs),
        ),
        compiler_params=pltpu.CompilerParams(vmem_limit_bytes=HOP_VMEM),
        name="last",
    )(meta, sizes, *owns, *msgs, occ, vir)


def body(ladder_ints, amplitudes, group_sizes, occ_energy, vir_energy):
    place = lax.axis_index("cd").astype(jnp.int32)
    x, z, core = place // (NZ * NC), (place // NC) % NZ, place % NC
    meta = jnp.stack([x, z, core]).astype(jnp.int32)
    their_ints = shifted(ladder_ints, 0, 0, 1)
    slab = lax.all_gather(amplitudes.T, "ab", axis=0)
    parts, _, rows = slab.shape
    parts = parts // NC
    my_rows = lax.dynamic_slice_in_dim(slab, core * parts, parts, 0)
    their_rows = lax.dynamic_slice_in_dim(slab, (1 - core) * parts, parts, 0)
    got_rows = shifted(their_rows, 0, 0, 1)
    half = parts * rows
    own_a, kept_a = ladder(0, meta, group_sizes, my_rows, got_rows, ladder_ints, their_ints)
    def block_ax(p, group, s, meta):
        return p * (2 * NZ // group) + s

    def block_bz(p, group, s, meta):
        return s * NZ + p

    own_b, kept_b = ladder(1, meta, group_sizes, my_rows, got_rows, ladder_ints, their_ints)
    first_a = ring(meta, own_a, "x", 2 * NZ, block_ax)
    first_b = ring(meta, own_b, "z", 2 * NX, block_bz)
    bz = ring(meta, own_b, "z", 2 * NX, block_bz, first_b, first_a)
    ax = ring(meta, own_a, "x", 2 * NZ, block_ax, first_a)
    chunk = place // NC * (2 * UNIT)
    owner = lax.axis_index("ab") * ladder_ints.shape[2] + chunk
    vir = lax.dynamic_slice_in_dim(vir_energy, owner, 2 * UNIT, 1).T
    occ = lax.dynamic_slice_in_dim(occ_energy, core * half, half, 0)[None, :]
    *ax, vir, occ = lax.optimization_barrier((*ax, vir, occ))
    az = spread(meta, kept_a, ax, "z")
    bx = spread(meta, kept_b, bz, "x")
    mine, other = last(meta, group_sizes, [kept_a, kept_b], ax + az + bz + bx, occ, vir)
    got = shifted(other, 0, 0, 1)
    low = jnp.where(core == 0, mine, got)
    high = jnp.where(core == 0, got, mine)
    return jnp.concatenate([low, high], axis=1).T


def solution(mesh):
    placed = (P(None, "cd", "ab"), P("ab", "cd"), P(), P(), P())
    return jax.shard_map(
        body, mesh=mesh, in_specs=placed, out_specs=P(None, ("ab", "cd")), check_vma=False
    )
```

```python
import functools

import jax
import jax.numpy as jnp
from jax import lax
from jax.experimental import pallas as pl
from jax.experimental.pallas import tpu as pltpu
from jax.sharding import PartitionSpec as P

NIRREP = 8
NX, NZ, NC = 4, 8, 2
UNIT = 48
WIDE = 256
TILE = 256
LADDER_VMEM = 42 << 20
HOP_VMEM = 20 << 20
PEAK = 32700.0
STEPS = 128.0
ROUND = 12582912.0
LEAST = 2.0**-100


def permutation(dx, dz, dc):
    def at(x, z, c):
        return ((x % NX) * NZ + z % NZ) * NC + c % NC

    return [
        (at(x, z, c), at(x + dx, z + dz, c + dc))
        for x in range(NX)
        for z in range(NZ)
        for c in range(NC)
    ]


def shifted(value, dx, dz, dc):
    return lax.ppermute(value, "cd", permutation(dx, dz, dc))


def span(meta, start, rows):
    end, low, high = jnp.int32(0), jnp.int32(0), jnp.int32(0)
    for g in range(NIRREP - 1):
        end = end + meta[3 + g]
        low = low + (end <= start).astype(jnp.int32)
        high = high + (end < start + rows).astype(jnp.int32)
    return low, high


def ladder_kernel(part, meta, t0_ref, t1_ref, v0_ref, v1_ref, out_ref, kept_ref, total_ref, sem, kept_sem):
    width, rows = total_ref.shape
    g = pl.program_id(0)
    first = jnp.int32(0)
    for k in range(NIRREP - 1):
        first = first + jnp.where(k < g, meta[3 + k], 0)
    last = first + meta[3 + g]
    base = meta[2] * (2 * rows) + part * rows
    pieces = [slice(j * WIDE, (j + 1) * WIDE) for j in range(width // WIDE)]
    tiles = [slice(q * TILE, (q + 1) * TILE) for q in range(rows // TILE)]

    def copy(q):
        return pltpu.make_async_copy(total_ref.at[:, tiles[q]], out_ref.at[:, tiles[q]], sem.at[q])

    for q, tile in enumerate(tiles):
        begin = base + q * TILE
        slab = (0, slice(None), tile)

        def product(piece, slab=slab):
            table = jnp.concatenate([v0_ref[0, :, piece], v1_ref[0, :, piece]], axis=0)
            both = jnp.concatenate([t0_ref[slab], t1_ref[slab]], axis=0)
            return lax.dot_general(table, both, (((0,), (0,)), ((), ())), preferred_element_type=jnp.float32)

        @pl.when((first <= begin) & (last > begin))
        def _(tile=tile, product=product):
            for piece in pieces:
                total_ref[piece, tile] = product(piece)

        @pl.when((first > begin) & (first < begin + TILE) & (last > first))
        def _(tile=tile, product=product, begin=begin):
            ids = begin + lax.broadcasted_iota(jnp.int32, (1, TILE), 1)
            for piece in pieces:
                total_ref[piece, tile] = jnp.where(ids >= first, product(piece), total_ref[piece, tile])

        @pl.when((first < begin + TILE) & (last >= begin + TILE))
        def _(q=q):
            copy(q).start()

    @pl.when(g == NIRREP - 1)
    def _():
        count = 1 if part == 0 else NX
        size = kept_ref.shape[0] // count
        copies = []
        for k in range(count):
            source = meta[0] * size if part == 0 else (k * NZ + meta[1]) * size
            rows_from = pl.ds(pl.multiple_of(source, 2 * UNIT), size)
            copies.append(
                pltpu.make_async_copy(total_ref.at[rows_from], kept_ref.at[pl.ds(k * size, size)], kept_sem.at[k])
            )
        for c in copies:
            c.start()
        for q in range(len(tiles)):
            copy(q).wait()
        for c in copies:
            c.wait()


def ladder(part, meta, t0, t1, v0, v1):
    depth, width = v0.shape[1:]
    rows = t0.shape[2]
    kept = width // (NX if part == 0 else NZ)

    def table(g, meta):
        low, high = span(meta, meta[2] * (2 * rows) + part * rows, rows)
        return jnp.minimum(jnp.maximum(g, low), high), 0, 0

    spec_t = pl.BlockSpec((1, depth, rows), lambda g, *_: (part, 0, 0))
    spec_v = pl.BlockSpec((1, depth, width), table)
    return pl.pallas_call(
        functools.partial(ladder_kernel, part),
        out_shape=[jax.ShapeDtypeStruct((n, rows), jnp.float32) for n in (width, kept)],
        grid_spec=pltpu.PrefetchScalarGridSpec(
            num_scalar_prefetch=1,
            grid=(NIRREP,),
            in_specs=[spec_t, spec_t, spec_v, spec_v],
            out_specs=[pl.BlockSpec(memory_space=pl.ANY)] * 2,
            scratch_shapes=[
                pltpu.VMEM((width, rows), jnp.float32),
                pltpu.SemaphoreType.DMA((rows // TILE,)),
                pltpu.SemaphoreType.DMA((NX,)),
            ],
        ),
        compiler_params=pltpu.CompilerParams(vmem_limit_bytes=LADDER_VMEM),
        cost_estimate=pl.CostEstimate(
            flops=8 * rows * depth * width, bytes_accessed=30 << 20, transcendentals=0
        ),
        name="ladder",
    )(meta, t0, t1, v0, v1)


def scale_of(code):
    return jnp.exp2(code * (1.0 / STEPS)) * (1.0 / PEAK)


def decode_scales(message_ref, scales_ref):
    n = message_ref.shape[0] // UNIT
    scales_ref[...] = scale_of(message_ref[n * UNIT : n * UNIT + 16, :].astype(jnp.float32))


def received(message_ref, scales_ref, unit):
    at = jnp.maximum(unit, 0)
    factor = jnp.where(unit >= 0, 1.0, 0.0)
    values = message_ref[pl.ds(pl.multiple_of(at * UNIT, 16), UNIT), :].astype(jnp.float32)
    return values * (scales_ref[pl.ds(at, 1), :] * factor)


def encoded(value):
    most = jnp.maximum(jnp.max(jnp.abs(value), axis=0, keepdims=True), LEAST)
    code = jnp.floor(jnp.log2(most) * STEPS) + 2.0
    coded = value * (1.0 / scale_of(code))
    coded = (coded + ROUND) - ROUND
    return coded.astype(jnp.int32).astype(jnp.int16), code


def hop_kernel(n, group, units, n_msgs, meta, *refs):
    own_refs, refs = refs[:2], refs[2:]
    msg_refs, refs = refs[:n_msgs], refs[n_msgs:]
    out_refs, refs = refs[:2], refs[2:]
    code_refs, scale_refs = refs[:2], refs[2:]
    step = pl.program_id(0)

    @pl.when(step == 0)
    def _():
        for m, s in zip(msg_refs, scale_refs):
            decode_scales(m, s)
        for c in code_refs:
            c[...] = jnp.zeros_like(c)

    for d in range(2):
        for k in range(group):
            i = step * group + k
            value = own_refs[d][k * UNIT : (k + 1) * UNIT, :]
            for j, unit in units(d, i, meta):
                value = value + received(msg_refs[j], scale_refs[j], unit)
            coded, code = encoded(value)
            rows = pl.ds(pl.multiple_of(i * UNIT, 16), UNIT)
            out_refs[d][rows, :] = coded
            code_refs[d][pl.ds(i, 1), :] = code

    @pl.when(step == n // group - 1)
    def _():
        for d in range(2):
            codes = code_refs[d][...].astype(jnp.int32).astype(jnp.int16)
            out_refs[d][n * UNIT : n * UNIT + 16, :] = codes


def hop(meta, own, msgs, n, group, block, units):
    rows = own.shape[1]

    def own_spec(d):
        return pl.BlockSpec((group * UNIT, rows), lambda s, meta: (block(d, s, meta), 0))

    def whole(shape):
        return pl.BlockSpec(shape, lambda s, meta: (0, 0))

    shape = (n * UNIT + 16, rows)
    return pl.pallas_call(
        functools.partial(hop_kernel, n, group, units, len(msgs)),
        out_shape=[jax.ShapeDtypeStruct(shape, jnp.int16)] * 2,
        grid_spec=pltpu.PrefetchScalarGridSpec(
            num_scalar_prefetch=1,
            grid=(n // group,),
            in_specs=[own_spec(0), own_spec(1)] + [whole(m.shape) for m in msgs],
            out_specs=[whole(shape)] * 2,
            scratch_shapes=[pltpu.VMEM((16, rows), jnp.float32)] * (2 + len(msgs)),
        ),
        compiler_params=pltpu.CompilerParams(vmem_limit_bytes=HOP_VMEM),
        cost_estimate=pl.CostEstimate(
            flops=20 * n * UNIT * rows, bytes_accessed=16 * n * UNIT * rows, transcendentals=0
        ),
        name="hop",
    )(meta, own, own, *msgs)


def both_ways(pair, axis):
    dx, dz = (1, 0) if axis == "x" else (0, 1)
    return [shifted(pair[0], dx, dz, 0), shifted(pair[1], -dx, -dz, 0)]


def ring(meta, own, axis, count, block_of, made=None, after=()):
    size, here = (NX, 0) if axis == "x" else (NZ, 1)
    sign = (1, -1)
    moving = []
    for step in range(size // 2):
        ahead = size // 2 - step
        halved = step == 0
        n = count // 2 if halved else count
        group = 4 if count == 16 else 2

        def place(d, meta, ahead=ahead):
            return (meta[here] + sign[d] * ahead + size) & (size - 1)

        def block(d, s, meta, group=group, halved=halved, place=place):
            skip = d * (count // 2 // group) if halved else 0
            return block_of(place(d, meta), group, s + skip, meta)

        def units(d, i, meta, step=step):
            if step == 0:
                return []
            if step > 1:
                return [(d, i)]
            half = count // 2
            return [(d, jnp.where(i < half, i, -1) if d == 0 else jnp.where(i >= half, i - half, -1))]

        if step == 0 and made is None:
            return hop(meta, own, moving, n, group, block, units)
        if step == 1:
            moving = lax.optimization_barrier((*moving, *after))[:2]
        moving = both_ways(made if step == 0 else hop(meta, own, moving, n, group, block, units), axis)
    return moving


def spread_kernel(size, here, meta, own_ref, *refs):
    msg_refs, out_refs, (here_ref, code_ref, *scale_refs) = refs[:2], refs[2 : size + 1], refs[size + 1 :]
    for m, s in zip(msg_refs, scale_refs):
        decode_scales(m, s)
    code_ref[...] = jnp.zeros_like(code_ref)

    def partial_sum(place, k):
        unit = 2 * place + k
        value = own_ref[pl.ds(pl.multiple_of(unit * UNIT, 16), UNIT), :]
        for m, s in zip(msg_refs, scale_refs):
            value = value + received(m, s, unit)
        return value

    for k in range(2):
        here_ref[k * UNIT : (k + 1) * UNIT, :] = partial_sum(meta[here], k)
    for d, out_ref in enumerate(out_refs):
        place = (meta[here] + d + 1) & (size - 1)
        for k in range(2):
            value = partial_sum(place, k)
            out_ref[k * UNIT : (k + 1) * UNIT, :], code_ref[k : k + 1, :] = encoded(value)
        out_ref[2 * UNIT :, :] = code_ref[...].astype(jnp.int32).astype(jnp.int16)


def spread(meta, own, msgs, axis):
    size, here = (NX, 0) if axis == "x" else (NZ, 1)
    rows = own.shape[1]
    shape = (2 * UNIT + 16, rows)

    def whole(shape):
        return pl.BlockSpec(shape, lambda s, meta: (0, 0))

    *out, stays = pl.pallas_call(
        functools.partial(spread_kernel, size, here),
        out_shape=[jax.ShapeDtypeStruct(shape, jnp.int16)] * (size - 1)
        + [jax.ShapeDtypeStruct((2 * UNIT, rows), jnp.float32)],
        grid_spec=pltpu.PrefetchScalarGridSpec(
            num_scalar_prefetch=1,
            grid=(1,),
            in_specs=[whole(a.shape) for a in (own, *msgs)],
            out_specs=[whole(shape)] * (size - 1) + [whole((2 * UNIT, rows))],
            scratch_shapes=[pltpu.VMEM((16, rows), jnp.float32)] * 3,
        ),
        compiler_params=pltpu.CompilerParams(vmem_limit_bytes=HOP_VMEM),
        name="spread",
    )(meta, own, *msgs)
    return stays, [shifted(m, *((d + 1, 0) if axis == "x" else (0, d + 1)), 0) for d, m in enumerate(out)]


def last_kernel(n_parts, meta, *refs):
    own_refs, refs = refs[:n_parts], refs[n_parts:]
    n_msgs = (len(refs) - 4) // 2
    msg_refs, refs = refs[:n_msgs], refs[n_msgs:]
    parts = (NZ - 1, NX - 1)
    occ_ref, vir_ref, mine_ref, other_ref = refs[:4]
    scale_refs = refs[4:]
    core = meta[2]
    rows = own_refs[0].shape[1]
    for m, s in zip(msg_refs, scale_refs):
        decode_scales(m, s)
    for p in range(n_parts):
        ids = core * (n_parts * rows) + p * rows + lax.broadcasted_iota(jnp.int32, (1, rows), 1)
        for out_ref, c in ((mine_ref, core), (other_ref, 1 - core)):
            at = pl.ds(pl.multiple_of(c * UNIT, 16), UNIT)
            total = own_refs[p][at, :]
            for j in range(sum(parts[:p]), sum(parts[: p + 1])):
                total = total + received(msg_refs[j], scale_refs[j], c)
            vir = jnp.zeros((UNIT, rows), jnp.float32)
            first = jnp.int32(0)
            for g in range(NIRREP):
                last = first + meta[3 + g]
                vir = jnp.where((ids >= first) & (ids < last), vir_ref[at, g : g + 1], vir)
                first = last
            cols = slice(p * rows, (p + 1) * rows)
            out_ref[:, cols] = (total / (occ_ref[:, cols] - vir)).astype(jnp.bfloat16)


def last(meta, owns, msgs, occ, vir):
    rows = owns[0].shape[1]

    def whole(shape):
        return pl.BlockSpec(shape, lambda s, meta: (0, 0))

    shape = (UNIT, len(owns) * rows)
    return pl.pallas_call(
        functools.partial(last_kernel, len(owns)),
        out_shape=[jax.ShapeDtypeStruct(shape, jnp.bfloat16)] * 2,
        grid_spec=pltpu.PrefetchScalarGridSpec(
            num_scalar_prefetch=1,
            grid=(1,),
            in_specs=[whole(a.shape) for a in (*owns, *msgs, occ, vir)],
            out_specs=[whole(shape)] * 2,
            scratch_shapes=[pltpu.VMEM((16, rows), jnp.float32)] * len(msgs),
        ),
        compiler_params=pltpu.CompilerParams(vmem_limit_bytes=HOP_VMEM),
        name="last",
    )(meta, *owns, *msgs, occ, vir)


def body(ladder_ints, amplitudes, group_sizes, occ_energy, vir_energy):
    place = lax.axis_index("cd").astype(jnp.int32)
    x, z, core = place // (NZ * NC), (place // NC) % NZ, place % NC
    meta = jnp.concatenate([jnp.stack([x, z, core]), group_sizes])
    their_ints = shifted(ladder_ints, 0, 0, 1)
    slab = lax.all_gather(amplitudes.T, "ab", axis=0)
    parts, _, rows = slab.shape
    parts = parts // NC
    my_rows = lax.dynamic_slice_in_dim(slab, core * parts, parts, 0)
    their_rows = lax.dynamic_slice_in_dim(slab, (1 - core) * parts, parts, 0)
    got_rows = shifted(their_rows, 0, 0, 1)
    half = parts * rows
    own_a, kept_a = ladder(0, meta, my_rows, got_rows, ladder_ints, their_ints)
    def block_ax(p, group, s, meta):
        return p * (2 * NZ // group) + s

    def block_bz(p, group, s, meta):
        return s * NZ + p

    own_b, kept_b = ladder(1, meta, my_rows, got_rows, ladder_ints, their_ints)
    first_a = ring(meta, own_a, "x", 2 * NZ, block_ax)
    first_b = ring(meta, own_b, "z", 2 * NX, block_bz)
    bz = ring(meta, own_b, "z", 2 * NX, block_bz, first_b, first_a)
    ax = ring(meta, own_a, "x", 2 * NZ, block_ax, first_a)
    chunk = place // NC * (2 * UNIT)
    owner = lax.axis_index("ab") * ladder_ints.shape[2] + chunk
    vir = lax.dynamic_slice_in_dim(vir_energy, owner, 2 * UNIT, 1).T
    occ = lax.dynamic_slice_in_dim(occ_energy, core * half, half, 0)[None, :]
    *ax, vir, occ = lax.optimization_barrier((*ax, vir, occ))
    stays_a, az = spread(meta, kept_a, ax, "z")
    stays_b, bx = spread(meta, kept_b, bz, "x")
    mine, other = last(meta, [stays_a, stays_b], az + bx, occ, vir)
    got = shifted(other, 0, 0, 1)
    both = [jnp.concatenate(pair, axis=1) for pair in ((mine, got), (got, mine))]
    return jnp.where(core == 0, *both).T


def solution(mesh):
    placed = (P(None, "cd", "ab"), P("ab", "cd"), P(), P(), P())
    return jax.shard_map(
        body, mesh=mesh, in_specs=placed, out_specs=P(None, ("ab", "cd")), check_vma=False
    )
```

```python
import functools

import jax
import jax.numpy as jnp
from jax import lax
from jax.experimental import pallas as pl
from jax.experimental.pallas import tpu as pltpu
from jax.sharding import PartitionSpec as P

NIRREP = 8
NX, NZ, NC = 4, 8, 2
UNIT = 48
WIDE = 256
TILE = 256
LADDER_VMEM = 42 << 20
HOP_VMEM = 20 << 20
PEAK = 32700.0
STEPS = 128.0
ROUND = 12582912.0
LEAST = 2.0**-100


def permutation(dx, dz, dc):
    def at(x, z, c):
        return ((x % NX) * NZ + z % NZ) * NC + c % NC

    return [
        (at(x, z, c), at(x + dx, z + dz, c + dc))
        for x in range(NX)
        for z in range(NZ)
        for c in range(NC)
    ]


def shifted(value, dx, dz, dc):
    return lax.ppermute(value, "cd", permutation(dx, dz, dc))


def span(meta, start, rows):
    end, low, high = jnp.int32(0), jnp.int32(0), jnp.int32(0)
    for g in range(NIRREP - 1):
        end = end + meta[3 + g]
        low = low + (end <= start).astype(jnp.int32)
        high = high + (end < start + rows).astype(jnp.int32)
    return low, high


def ladder_kernel(part, meta, t0_ref, t1_ref, v0_ref, v1_ref, out_ref, kept_ref, total_ref, sem, kept_sem):
    width, rows = total_ref.shape
    g = pl.program_id(0)
    first = jnp.int32(0)
    for k in range(NIRREP - 1):
        first = first + jnp.where(k < g, meta[3 + k], 0)
    last = first + meta[3 + g]
    base = meta[2] * (2 * rows) + part * rows
    pieces = [slice(j * WIDE, (j + 1) * WIDE) for j in range(width // WIDE)]
    tiles = [slice(q * TILE, (q + 1) * TILE) for q in range(rows // TILE)]

    def copy(q):
        return pltpu.make_async_copy(total_ref.at[:, tiles[q]], out_ref.at[:, tiles[q]], sem.at[q])

    for q, tile in enumerate(tiles):
        begin = base + q * TILE
        slab = (0, slice(None), tile)

        def product(piece, slab=slab):
            table = jnp.concatenate([v0_ref[0, :, piece], v1_ref[0, :, piece]], axis=0)
            both = jnp.concatenate([t0_ref[slab], t1_ref[slab]], axis=0)
            return lax.dot_general(table, both, (((0,), (0,)), ((), ())), preferred_element_type=jnp.float32)

        @pl.when((first <= begin) & (last > begin))
        def _(tile=tile, product=product):
            for piece in pieces:
                total_ref[piece, tile] = product(piece)

        @pl.when((first > begin) & (first < begin + TILE) & (last > first))
        def _(tile=tile, product=product, begin=begin):
            ids = begin + lax.broadcasted_iota(jnp.int32, (1, TILE), 1)
            for piece in pieces:
                total_ref[piece, tile] = jnp.where(ids >= first, product(piece), total_ref[piece, tile])

        @pl.when((first < begin + TILE) & (last >= begin + TILE))
        def _(q=q):
            copy(q).start()

    @pl.when(g == NIRREP - 1)
    def _():
        count = 1 if part == 0 else NX
        size = kept_ref.shape[0] // count
        copies = []
        for k in range(count):
            source = meta[0] * size if part == 0 else (k * NZ + meta[1]) * size
            rows_from = pl.ds(pl.multiple_of(source, 2 * UNIT), size)
            copies.append(
                pltpu.make_async_copy(total_ref.at[rows_from], kept_ref.at[pl.ds(k * size, size)], kept_sem.at[k])
            )
        for c in copies:
            c.start()
        for q in range(len(tiles)):
            copy(q).wait()
        for c in copies:
            c.wait()


def ladder(part, meta, t0, t1, v0, v1):
    depth, width = v0.shape[1:]
    rows = t0.shape[2]
    kept = width // (NX if part == 0 else NZ)

    def table(g, meta):
        low, high = span(meta, meta[2] * (2 * rows) + part * rows, rows)
        return jnp.minimum(jnp.maximum(g, low), high), 0, 0

    spec_t = pl.BlockSpec((1, depth, rows), lambda g, *_: (part, 0, 0))
    spec_v = pl.BlockSpec((1, depth, width), table)
    return pl.pallas_call(
        functools.partial(ladder_kernel, part),
        out_shape=[jax.ShapeDtypeStruct((n, rows), jnp.float32) for n in (width, kept)],
        grid_spec=pltpu.PrefetchScalarGridSpec(
            num_scalar_prefetch=1,
            grid=(NIRREP,),
            in_specs=[spec_t, spec_t, spec_v, spec_v],
            out_specs=[pl.BlockSpec(memory_space=pl.ANY)] * 2,
            scratch_shapes=[
                pltpu.VMEM((width, rows), jnp.float32),
                pltpu.SemaphoreType.DMA((rows // TILE,)),
                pltpu.SemaphoreType.DMA((NX,)),
            ],
        ),
        compiler_params=pltpu.CompilerParams(vmem_limit_bytes=LADDER_VMEM),
        cost_estimate=pl.CostEstimate(
            flops=8 * rows * depth * width, bytes_accessed=30 << 20, transcendentals=0
        ),
        name="ladder",
    )(meta, t0, t1, v0, v1)


def scale_of(code):
    return jnp.exp2(code * (1.0 / STEPS)) * (1.0 / PEAK)


def decode_scales(message_ref, scales_ref):
    n = message_ref.shape[0] // UNIT
    scales_ref[...] = scale_of(message_ref[n * UNIT : n * UNIT + 16, :].astype(jnp.float32))


def received(message_ref, scales_ref, unit):
    at = jnp.maximum(unit, 0)
    factor = jnp.where(unit >= 0, 1.0, 0.0)
    values = message_ref[pl.ds(pl.multiple_of(at * UNIT, 16), UNIT), :].astype(jnp.float32)
    return values * (scales_ref[pl.ds(at, 1), :] * factor)


def encoded(value):
    most = jnp.maximum(jnp.max(jnp.abs(value), axis=0, keepdims=True), LEAST)
    code = jnp.floor(jnp.log2(most) * STEPS) + 2.0
    coded = value * (1.0 / scale_of(code))
    coded = (coded + ROUND) - ROUND
    return coded.astype(jnp.int32).astype(jnp.int16), code


def hop_kernel(n, group, units, n_msgs, meta, *refs):
    own_refs, refs = refs[:2], refs[2:]
    msg_refs, refs = refs[:n_msgs], refs[n_msgs:]
    out_refs, refs = refs[:2], refs[2:]
    code_refs, scale_refs = refs[:2], refs[2:]
    step = pl.program_id(0)

    @pl.when(step == 0)
    def _():
        for m, s in zip(msg_refs, scale_refs):
            decode_scales(m, s)
        for c in code_refs:
            c[...] = jnp.zeros_like(c)

    for d in range(2):
        for k in range(group):
            i = step * group + k
            value = own_refs[d][k * UNIT : (k + 1) * UNIT, :]
            for j, unit in units(d, i, meta):
                value = value + received(msg_refs[j], scale_refs[j], unit)
            coded, code = encoded(value)
            rows = pl.ds(pl.multiple_of(i * UNIT, 16), UNIT)
            out_refs[d][rows, :] = coded
            code_refs[d][pl.ds(i, 1), :] = code

    @pl.when(step == n // group - 1)
    def _():
        for d in range(2):
            codes = code_refs[d][...].astype(jnp.int32).astype(jnp.int16)
            out_refs[d][n * UNIT : n * UNIT + 16, :] = codes


def hop(meta, own, msgs, n, group, block, units):
    rows = own.shape[1]

    def own_spec(d):
        return pl.BlockSpec((group * UNIT, rows), lambda s, meta: (block(d, s, meta), 0))

    def whole(shape):
        return pl.BlockSpec(shape, lambda s, meta: (0, 0))

    shape = (n * UNIT + 16, rows)
    return pl.pallas_call(
        functools.partial(hop_kernel, n, group, units, len(msgs)),
        out_shape=[jax.ShapeDtypeStruct(shape, jnp.int16)] * 2,
        grid_spec=pltpu.PrefetchScalarGridSpec(
            num_scalar_prefetch=1,
            grid=(n // group,),
            in_specs=[own_spec(0), own_spec(1)] + [whole(m.shape) for m in msgs],
            out_specs=[whole(shape)] * 2,
            scratch_shapes=[pltpu.VMEM((16, rows), jnp.float32)] * (2 + len(msgs)),
        ),
        compiler_params=pltpu.CompilerParams(vmem_limit_bytes=HOP_VMEM),
        cost_estimate=pl.CostEstimate(
            flops=20 * n * UNIT * rows, bytes_accessed=16 * n * UNIT * rows, transcendentals=0
        ),
        name="hop",
    )(meta, own, own, *msgs)


def both_ways(pair, axis):
    dx, dz = (1, 0) if axis == "x" else (0, 1)
    return [shifted(pair[0], dx, dz, 0), shifted(pair[1], -dx, -dz, 0)]


def ring_step(meta, own, axis, count, block_of, step, moving=()):
    size, here = (NX, 0) if axis == "x" else (NZ, 1)
    sign = (1, -1)
    ahead = size // 2 - step
    halved = step == 0
    n = count // 2 if halved else count
    group = 4 if count == 16 else 2

    def place(d, meta, ahead=ahead):
        return (meta[here] + sign[d] * ahead + size) & (size - 1)

    def block(d, s, meta, group=group, halved=halved, place=place):
        skip = d * (count // 2 // group) if halved else 0
        return block_of(place(d, meta), group, s + skip, meta)

    def units(d, i, meta, step=step):
        if step == 0:
            return []
        if step > 1:
            return [(d, i)]
        half = count // 2
        return [(d, jnp.where(i < half, i, -1) if d == 0 else jnp.where(i >= half, i - half, -1))]

    return hop(meta, own, moving, n, group, block, units)


def spread_kernel(size, here, meta, own_ref, *refs):
    msg_refs, out_refs, (here_ref, code_ref, *scale_refs) = refs[:2], refs[2 : size + 1], refs[size + 1 :]
    for m, s in zip(msg_refs, scale_refs):
        decode_scales(m, s)
    code_ref[...] = jnp.zeros_like(code_ref)

    def partial_sum(place, k):
        unit = 2 * place + k
        value = own_ref[pl.ds(pl.multiple_of(unit * UNIT, 16), UNIT), :]
        for m, s in zip(msg_refs, scale_refs):
            value = value + received(m, s, unit)
        return value

    for k in range(2):
        here_ref[k * UNIT : (k + 1) * UNIT, :] = partial_sum(meta[here], k)
    for d, out_ref in enumerate(out_refs):
        place = (meta[here] + d + 1) & (size - 1)
        for k in range(2):
            value = partial_sum(place, k)
            out_ref[k * UNIT : (k + 1) * UNIT, :], code_ref[k : k + 1, :] = encoded(value)
        out_ref[2 * UNIT :, :] = code_ref[...].astype(jnp.int32).astype(jnp.int16)


def spread(meta, own, msgs, axis):
    size, here = (NX, 0) if axis == "x" else (NZ, 1)
    rows = own.shape[1]
    shape = (2 * UNIT + 16, rows)

    def whole(shape):
        return pl.BlockSpec(shape, lambda s, meta: (0, 0))

    *out, stays = pl.pallas_call(
        functools.partial(spread_kernel, size, here),
        out_shape=[jax.ShapeDtypeStruct(shape, jnp.int16)] * (size - 1)
        + [jax.ShapeDtypeStruct((2 * UNIT, rows), jnp.float32)],
        grid_spec=pltpu.PrefetchScalarGridSpec(
            num_scalar_prefetch=1,
            grid=(1,),
            in_specs=[whole(a.shape) for a in (own, *msgs)],
            out_specs=[whole(shape)] * (size - 1) + [whole((2 * UNIT, rows))],
            scratch_shapes=[pltpu.VMEM((16, rows), jnp.float32)] * 3,
        ),
        compiler_params=pltpu.CompilerParams(vmem_limit_bytes=HOP_VMEM),
        name="spread",
    )(meta, own, *msgs)
    return stays, [shifted(m, *((d + 1, 0) if axis == "x" else (0, d + 1)), 0) for d, m in enumerate(out)]


def last_kernel(n_parts, meta, *refs):
    own_refs, refs = refs[:n_parts], refs[n_parts:]
    n_msgs = (len(refs) - 4) // 2
    msg_refs, refs = refs[:n_msgs], refs[n_msgs:]
    parts = (NZ - 1, NX - 1)
    occ_ref, vir_ref, mine_ref, other_ref = refs[:4]
    scale_refs = refs[4:]
    core = meta[2]
    rows = own_refs[0].shape[1]
    for m, s in zip(msg_refs, scale_refs):
        decode_scales(m, s)
    for p in range(n_parts):
        ids = core * (n_parts * rows) + p * rows + lax.broadcasted_iota(jnp.int32, (1, rows), 1)
        for out_ref, c in ((mine_ref, core), (other_ref, 1 - core)):
            at = pl.ds(pl.multiple_of(c * UNIT, 16), UNIT)
            total = own_refs[p][at, :]
            for j in range(sum(parts[:p]), sum(parts[: p + 1])):
                total = total + received(msg_refs[j], scale_refs[j], c)
            vir = jnp.zeros((UNIT, rows), jnp.float32)
            first = jnp.int32(0)
            for g in range(NIRREP):
                last = first + meta[3 + g]
                vir = jnp.where((ids >= first) & (ids < last), vir_ref[at, g : g + 1], vir)
                first = last
            cols = slice(p * rows, (p + 1) * rows)
            out_ref[:, cols] = (total / (occ_ref[:, cols] - vir)).astype(jnp.bfloat16)


def last(meta, owns, msgs, occ, vir):
    rows = owns[0].shape[1]

    def whole(shape):
        return pl.BlockSpec(shape, lambda s, meta: (0, 0))

    shape = (UNIT, len(owns) * rows)
    return pl.pallas_call(
        functools.partial(last_kernel, len(owns)),
        out_shape=[jax.ShapeDtypeStruct(shape, jnp.bfloat16)] * 2,
        grid_spec=pltpu.PrefetchScalarGridSpec(
            num_scalar_prefetch=1,
            grid=(1,),
            in_specs=[whole(a.shape) for a in (*owns, *msgs, occ, vir)],
            out_specs=[whole(shape)] * 2,
            scratch_shapes=[pltpu.VMEM((16, rows), jnp.float32)] * len(msgs),
        ),
        compiler_params=pltpu.CompilerParams(vmem_limit_bytes=HOP_VMEM),
        name="last",
    )(meta, *owns, *msgs, occ, vir)


def body(ladder_ints, amplitudes, group_sizes, occ_energy, vir_energy):
    place = lax.axis_index("cd").astype(jnp.int32)
    x, z, core = place // (NZ * NC), (place // NC) % NZ, place % NC
    meta = jnp.concatenate([jnp.stack([x, z, core]), group_sizes])
    their_ints = shifted(ladder_ints, 0, 0, 1)
    slab = lax.all_gather(amplitudes.T, "ab", axis=0)
    parts, _, rows = slab.shape
    parts = parts // NC
    my_rows = lax.dynamic_slice_in_dim(slab, core * parts, parts, 0)
    their_rows = lax.dynamic_slice_in_dim(slab, (1 - core) * parts, parts, 0)
    got_rows = shifted(their_rows, 0, 0, 1)
    half = parts * rows
    own_a, kept_a = ladder(0, meta, my_rows, got_rows, ladder_ints, their_ints)
    def block_ax(p, group, s, meta):
        return p * (2 * NZ // group) + s

    def block_bz(p, group, s, meta):
        return s * NZ + p

    step_a = functools.partial(ring_step, meta, own_a, "x", 2 * NZ, block_ax)
    own_b, kept_b = ladder(1, meta, my_rows, got_rows, ladder_ints, their_ints)
    ax = both_ways(step_a(1, both_ways(step_a(0), "x")), "x")
    bz = ()
    for step in range(NZ // 2):
        if step == NZ // 2 - 1:
            bz = lax.optimization_barrier((*bz, *ax))[:2]
        bz = both_ways(ring_step(meta, own_b, "z", 2 * NX, block_bz, step, bz), "z")
    chunk = place // NC * (2 * UNIT)
    owner = lax.axis_index("ab") * ladder_ints.shape[2] + chunk
    vir = lax.dynamic_slice_in_dim(vir_energy, owner, 2 * UNIT, 1).T
    occ = lax.dynamic_slice_in_dim(occ_energy, core * half, half, 0)[None, :]
    *ax, vir, occ = lax.optimization_barrier((*ax, vir, occ))
    stays_a, az = spread(meta, kept_a, ax, "z")
    stays_b, bx = spread(meta, kept_b, bz, "x")
    mine, other = last(meta, [stays_a, stays_b], az + bx, occ, vir)
    got = shifted(other, 0, 0, 1)
    both = [jnp.concatenate(pair, axis=1) for pair in ((mine, got), (got, mine))]
    return jnp.where(core == 0, *both).T


def solution(mesh):
    placed = (P(None, "cd", "ab"), P("ab", "cd"), P(), P(), P())
    return jax.shard_map(
        body, mesh=mesh, in_specs=placed, out_specs=P(None, ("ab", "cd")), check_vma=False
    )
```
